32 devices in a mesh: seq: 2 (over x), dp: 4 (over z), fsdp: 4 (over y, core).
Axes of the slice: x: 2, y: 2, z: 4, core: 2. Of those that a mesh axis runs over, the one named last changes fastest.
Arguments:
- query_rows: bfloat16 [16, 256, 4096], P(('dp', 'fsdp'), 'seq'), may hold values from -2.5 to 2.5
- forward_key_rows: bfloat16 [16, 256, 1024], P(('dp', 'fsdp'), 'seq'), may hold values from -2.5 to 2.5
- forward_value_rows: bfloat16 [16, 256, 1024], P(('dp', 'fsdp'), 'seq'), may hold values from -4 to 4
- out_cotangent: bfloat16 [16, 256, 4096], P(('dp', 'fsdp'), 'seq'), may hold values from -4 to 4
- proj_weight: bfloat16 [4096, 4096], P(('dp', 'fsdp'), 'seq'), may hold values from -0.09375 to 0.09375
- sent_lengths: int32 [16, 8], P(('dp', 'fsdp')), may hold values from 1 to 64, 256 in all within a row
Outputs:
- query_grad: bfloat16 [16, 256, 4096], P(('dp', 'fsdp'), 'seq')
- key_gradient: bfloat16 [16, 256, 1024], P(('dp', 'fsdp'), 'seq')
- value_gradient: bfloat16 [16, 256, 1024], P(('dp', 'fsdp'), 'seq')
- proj_grad: bfloat16 [4096, 4096], P(('dp', 'fsdp'), 'seq')
The draws below stay inside these ranges and needn't reach their ends.
Inputs may be any that keep to these rules, and one draw needn't show every extreme that they name: `sent_lengths`: each window's 8 lengths sum to 256, and the longest is exactly 64.
All inputs are finite; a program needn't handle non-finite values.
Results may differ from the reference program's by a relative error of at most 0.0058.
Values may be sent and summed in bfloat16 or wider, within the bound.
A program may use at most 128 MiB of HBM per device.

```python
import math
import jax
import jax.numpy as jnp
import numpy as np
from jax import lax

D = 4096
QUERY_HEADS = 32
KEY_VALUE_HEADS = 8
HEAD_SIZE = 128
WINDOW_LENGTH = 256
SENTS = 8
MOST = 64
WINDOW_COUNT = 16


def spiked(array, own_key, source, target, blocks, factor):
    owner, partner = [(jnp.arange(array.shape[dim]) // (array.shape[dim] // blocks)).reshape([-1 if axis == dim else 1 for axis in range(array.ndim)]) for dim in (source, target)]
    chosen = jax.random.permutation(own_key, blocks)[partner]
    strong = (owner == chosen) | (owner == (partner + blocks // 2) % blocks)
    return jnp.where(strong, factor * array, array)


def shard_levels(rng, extent, split, smallest, top_value):
    def one(axis_at, parts):
        draws = jax.random.uniform(jax.random.fold_in(jax.random.fold_in(rng, 6), axis_at), (parts,), jnp.float32, smallest / len(split), top_value / len(split))
        return jnp.repeat(jnp.exp(draws), extent[axis_at] // parts).reshape((-1,) + (1,) * (len(extent) - axis_at - 1))

    level = one(*split[0])
    for cut in split[1:]:
        level = level * one(*cut)
    return level


def split_up(amount, total, limit, lean):
    weights = [(1 << 20) // math.isqrt(grade ** lean) + 1 for grade in range(2, amount + 1)]
    surplus, holding = total - limit - (amount - 1), [1] * (amount - 1)
    while surplus > 0:
        free = [i for i in range(amount - 1) if holding[i] < limit]
        pool, budget = sum([weights[i] for i in free]), surplus
        for i in free:
            extra = min(limit - holding[i], max(1, budget * weights[i] // pool), surplus)
            holding[i] = holding[i] + extra
            surplus = surplus - extra
    return np.array([limit] + holding)


def uneven_parts(own_key, number_of, total, reach, lean):
    if number_of == 2:
        one = jax.random.randint(own_key, (), max(1, total - reach), min(reach, total - 1) + 1)
        return jnp.stack([one, total - one])
    sizes = jnp.asarray(split_up(number_of, total, reach, lean), jnp.int32)
    couples = (number_of - 1) // 2
    giver, receiver = sizes[1:1 + 2 * couples:2], sizes[2:2 + 2 * couples:2]
    room = jnp.minimum(giver - 1, reach - receiver)
    moved = jax.random.randint(jax.random.fold_in(own_key, 1), (couples,), 0, 1 << 20) % (room + 1)
    sizes = sizes.at[1:1 + 2 * couples:2].set(giver - moved).at[2:2 + 2 * couples:2].set(receiver + moved)
    return sizes[jax.random.permutation(jax.random.fold_in(own_key, 2), number_of)]


def centred(rng, shape, spread, limit, shards=(), held_as=jnp.bfloat16):
    drawn = spread * jax.random.normal(rng, shape, jnp.float32)
    if shards:
        drawn = drawn * shard_levels(rng, shape, shards, -0.22, 0.18)
    return jnp.clip(drawn, -limit, limit).astype(held_as)


def heavy_noise(key, extent, deviation, most, shards, heavy, kind=jnp.bfloat16):
    values = deviation * jax.random.normal(key, extent, jnp.float32)
    if shards:
        values = values * shard_levels(key, extent, shards, -0.22, 0.18)
    return jnp.clip(spiked(values, jax.random.fold_in(key, 3), *heavy), -most, most).astype(kind)


def setup_inputs(seed: int = 0) -> dict:
    key_list = jax.random.split(jax.random.key(seed), 7)
    query_rows = centred(key_list[0], (WINDOW_COUNT, WINDOW_LENGTH, QUERY_HEADS * HEAD_SIZE), 1.0, 2.5, ((0, 16), (1, 2)))
    forward_key_rows = centred(key_list[1], (WINDOW_COUNT, WINDOW_LENGTH, KEY_VALUE_HEADS * HEAD_SIZE), 1.0, 2.5, ((0, 16), (1, 2)))
    forward_value_rows = centred(key_list[2], (WINDOW_COUNT, WINDOW_LENGTH, KEY_VALUE_HEADS * HEAD_SIZE), 1.0, 4.0, ((0, 16), (1, 2)))
    out_cotangent = heavy_noise(key_list[3], (WINDOW_COUNT, WINDOW_LENGTH, D), 1.0, 4.0, ((0, 16), (1, 2)), (0, 2, 16, 2.0))
    proj_weight = centred(key_list[4], (D, QUERY_HEADS * HEAD_SIZE), (QUERY_HEADS * HEAD_SIZE) ** -0.5, 0.09375, ((0, 16), (1, 2)))
    sent_lengths = jax.vmap(lambda own: uneven_parts(own, SENTS, WINDOW_LENGTH, MOST, 1))(jax.random.split(key_list[5], WINDOW_COUNT)).reshape((WINDOW_COUNT, SENTS)).astype(jnp.int32)
    return dict(query_rows=query_rows, forward_key_rows=forward_key_rows, forward_value_rows=forward_value_rows, out_cotangent=out_cotangent, proj_weight=proj_weight, sent_lengths=sent_lengths)


def sentence_ids(length_row):
    bounds = jnp.cumsum(length_row).astype(jnp.int32)
    places = jnp.arange(WINDOW_LENGTH, dtype=jnp.int32)
    return lax.optimization_barrier(jnp.sum((places[:, None] >= bounds[None, :]).astype(jnp.int32), axis=1)).astype(jnp.int32)

def reference(query_rows, forward_key_rows, forward_value_rows, out_cotangent, proj_weight, sent_lengths):
    queries_per_group = QUERY_HEADS // KEY_VALUE_HEADS
    factor = 1.0 / math.sqrt(HEAD_SIZE)

    def window(running, inputs):
        query_matrix, every_key_row, every_value_row, cotangent, length_row = inputs
        sentence = sentence_ids(length_row)
        allowed = (sentence[None, :] <= sentence[:, None]) & (sentence[None, :] >= sentence[:, None] - 3)
        upstream_gradient = jnp.dot(cotangent, proj_weight, preferred_element_type=jnp.float32).astype(jnp.bfloat16)
        upstream_gradient = lax.optimization_barrier(upstream_gradient)
        heads_of_queries = query_matrix.reshape(WINDOW_LENGTH, KEY_VALUE_HEADS, queries_per_group, HEAD_SIZE).transpose(1, 2, 0, 3)
        heads_of_keys = every_key_row.reshape(WINDOW_LENGTH, KEY_VALUE_HEADS, HEAD_SIZE).transpose(1, 0, 2)
        heads_of_values = every_value_row.reshape(WINDOW_LENGTH, KEY_VALUE_HEADS, HEAD_SIZE).transpose(1, 0, 2)
        heads_of_upstream = upstream_gradient.reshape(WINDOW_LENGTH, KEY_VALUE_HEADS, queries_per_group, HEAD_SIZE).transpose(1, 2, 0, 3)

        def one_head(pieces):
            query_wide = pieces[0].astype(jnp.float32)
            key_wide = pieces[1].astype(jnp.float32)
            value_wide = pieces[2].astype(jnp.float32)
            upstream_wide = pieces[3].astype(jnp.float32)
            scores = jnp.einsum('hqd,kd->hqk', query_wide, key_wide) * factor
            raised = jnp.where(allowed[None], jnp.exp(scores), 0.0)
            attend = raised / lax.optimization_barrier(jnp.sum(raised, axis=-1, keepdims=True))
            rounded = lax.optimization_barrier(attend.astype(jnp.bfloat16)).astype(jnp.float32)
            output = jnp.einsum('hqk,kd->hqd', rounded, value_wide).astype(jnp.bfloat16)
            grad_attend = jnp.einsum('hqd,kd->hqk', upstream_wide, value_wide)
            dscore = attend * (grad_attend - lax.optimization_barrier(jnp.sum(attend * grad_attend, axis=-1, keepdims=True))) * factor
            dscore = lax.optimization_barrier(dscore.astype(jnp.bfloat16)).astype(jnp.float32)
            query_grad = jnp.einsum('hqk,kd->hqd', dscore, key_wide).astype(jnp.bfloat16)
            key_gradient = jnp.einsum('hqk,hqd->kd', dscore, query_wide).astype(jnp.bfloat16)
            value_gradient = jnp.einsum('hqk,hqd->kd', rounded, upstream_wide).astype(jnp.bfloat16)
            return (output, query_grad, key_gradient, value_gradient)
        result_list = lax.map(one_head, (heads_of_queries, heads_of_keys, heads_of_values, heads_of_upstream))
        output = result_list[0].transpose(2, 0, 1, 3).reshape(WINDOW_LENGTH, QUERY_HEADS * HEAD_SIZE)
        query_grad = result_list[1].transpose(2, 0, 1, 3).reshape(WINDOW_LENGTH, QUERY_HEADS * HEAD_SIZE)
        key_gradient = result_list[2].transpose(1, 0, 2).reshape(WINDOW_LENGTH, KEY_VALUE_HEADS * HEAD_SIZE)
        value_gradient = result_list[3].transpose(1, 0, 2).reshape(WINDOW_LENGTH, KEY_VALUE_HEADS * HEAD_SIZE)
        running = running + jnp.dot(cotangent.T, output, preferred_element_type=jnp.float32)
        return (running, (query_grad, key_gradient, value_gradient))
    starting = jnp.zeros((D, QUERY_HEADS * HEAD_SIZE), jnp.float32)
    summed, gradients = lax.scan(window, starting, (query_rows, forward_key_rows, forward_value_rows, out_cotangent, sent_lengths))
    return (gradients[0], gradients[1], gradients[2], summed.astype(jnp.bfloat16))
```

```python
import math

import jax
import jax.numpy as jnp
from jax import lax
from jax.experimental import pallas as pl
from jax.experimental.pallas import tpu as pltpu
from jax.sharding import PartitionSpec as P

QUERY_HEADS = 32
KEY_VALUE_HEADS = 8
HEAD_SIZE = 128


def running_sums(lengths):
    index = jnp.arange(lengths.shape[0], dtype=jnp.int32)
    return jnp.sum(jnp.where(index[None, :] <= index[:, None], lengths[None, :], 0), axis=1)


def per_device(
    query_rows, forward_key_rows, forward_value_rows, out_cotangent, proj_weight, sent_lengths
):
    queries_per_group = QUERY_HEADS // KEY_VALUE_HEADS
    factor = 1.0 / math.sqrt(HEAD_SIZE)
    gathered = lax.all_gather(out_cotangent, "seq", axis=1, tiled=True)
    cotangent = gathered[0]
    length = cotangent.shape[0]
    sliced = cotangent
    upstream_gradient = jnp.dot(
        sliced,
        lax.all_gather(proj_weight, ("dp", "fsdp"), axis=0, tiled=True),
        preferred_element_type=jnp.float32,
    ).astype(jnp.bfloat16)
    heads_of_queries, heads_of_keys, heads_of_values = (
        lax.all_to_all(query_rows, "seq", split_axis=2, concat_axis=1, tiled=True),
        lax.all_to_all(forward_key_rows, "seq", split_axis=2, concat_axis=1, tiled=True),
        lax.all_to_all(forward_value_rows, "seq", split_axis=2, concat_axis=1, tiled=True),
    )
    heads_of_queries = heads_of_queries[0]
    heads_of_keys = heads_of_keys[0]
    heads_of_values = heads_of_values[0]
    bounds = running_sums(sent_lengths[0])
    places = jnp.arange(length, dtype=jnp.int32)
    sentence = jnp.sum((places[:, None] >= bounds[None, :]).astype(jnp.int32), axis=1)
    block_rows = min(512, length)
    block_count = length // block_rows
    kv_local = heads_of_keys.shape[1] // HEAD_SIZE
    group_cols = queries_per_group * HEAD_SIZE
    output_parts = []
    query_parts = []
    key_parts = []
    value_parts = []
    for head_index in range(kv_local):
        key_head = heads_of_keys[:, head_index * HEAD_SIZE : (head_index + 1) * HEAD_SIZE]
        value_head = heads_of_values[:, head_index * HEAD_SIZE : (head_index + 1) * HEAD_SIZE]
        query_group = heads_of_queries[:, head_index * group_cols : (head_index + 1) * group_cols]
        upstream_group = upstream_gradient[
            :, head_index * group_cols : (head_index + 1) * group_cols
        ]

        def block_step(block_index, buffers):
            output_buf, query_buf, key_buf, value_buf = buffers
            offset = block_index * block_rows
            query_block = lax.dynamic_slice_in_dim(query_group, offset, block_rows, 0).reshape(
                block_rows, queries_per_group, HEAD_SIZE
            )
            upstream_block = lax.dynamic_slice_in_dim(
                upstream_group, offset, block_rows, 0
            ).reshape(block_rows, queries_per_group, HEAD_SIZE)
            sentence_query = lax.dynamic_slice_in_dim(sentence, offset, block_rows, 0)
            allowed = (sentence[None, :] <= sentence_query[:, None]) & (
                sentence[None, :] >= sentence_query[:, None] - 3
            )
            scores = (
                jnp.einsum("qhd,kd->hqk", query_block, key_head, preferred_element_type=jnp.float32)
                * factor
            )
            raised = jnp.where(allowed[None], jnp.exp(scores), 0.0)
            attend = raised / jnp.sum(raised, axis=-1, keepdims=True)
            rounded = attend.astype(jnp.bfloat16)
            output_block = jnp.einsum(
                "hqk,kd->qhd", rounded, value_head, preferred_element_type=jnp.float32
            ).astype(jnp.bfloat16)
            grad_attend = jnp.einsum(
                "qhd,kd->hqk", upstream_block, value_head, preferred_element_type=jnp.float32
            )
            dscore = (
                attend
                * (grad_attend - jnp.sum(attend * grad_attend, axis=-1, keepdims=True))
                * factor
            ).astype(jnp.bfloat16)
            query_block_grad = jnp.einsum(
                "hqk,kd->qhd", dscore, key_head, preferred_element_type=jnp.float32
            ).astype(jnp.bfloat16)
            key_window_grad = jnp.einsum(
                "hqk,qhd->kd", dscore, query_block, preferred_element_type=jnp.float32
            )
            value_window_grad = jnp.einsum(
                "hqk,qhd->kd", rounded, upstream_block, preferred_element_type=jnp.float32
            )
            output_buf = lax.dynamic_update_slice_in_dim(
                output_buf, output_block.reshape(block_rows, group_cols), offset, 0
            )
            query_buf = lax.dynamic_update_slice_in_dim(
                query_buf, query_block_grad.reshape(block_rows, group_cols), offset, 0
            )
            key_old = key_buf
            key_buf = key_old + key_window_grad
            value_old = value_buf
            value_buf = value_old + value_window_grad
            return (output_buf, query_buf, key_buf, value_buf)

        starting = (
            jnp.zeros((length, group_cols), jnp.bfloat16),
            jnp.zeros((length, group_cols), jnp.bfloat16),
            jnp.zeros((length, HEAD_SIZE), jnp.float32),
            jnp.zeros((length, HEAD_SIZE), jnp.float32),
        )
        output_buf, query_buf, key_buf, value_buf = lax.fori_loop(
            0, block_count, block_step, starting
        )
        output_parts.append(output_buf)
        query_parts.append(query_buf)
        key_parts.append(key_buf.astype(jnp.bfloat16))
        value_parts.append(value_buf.astype(jnp.bfloat16))
    output_all = jnp.concatenate(output_parts, axis=1)
    query_all = jnp.concatenate(query_parts, axis=1)
    key_all = jnp.concatenate(key_parts, axis=1)
    value_all = jnp.concatenate(value_parts, axis=1)
    sliced = cotangent
    proj_grad = lax.psum_scatter(
        lax.dot_general(
            sliced, output_all, (((0,), (0,)), ((), ())), preferred_element_type=jnp.float32
        ),
        ("dp", "fsdp"),
        scatter_dimension=0,
        tiled=True,
    ).astype(jnp.bfloat16)
    query_grad, key_gradient, value_gradient = (
        lax.all_to_all(query_all[None], "seq", split_axis=1, concat_axis=2, tiled=True),
        lax.all_to_all(key_all[None], "seq", split_axis=1, concat_axis=2, tiled=True),
        lax.all_to_all(value_all[None], "seq", split_axis=1, concat_axis=2, tiled=True),
    )
    return (query_grad, key_gradient, value_gradient, proj_grad)


MESH = pl.DeviceIdType.MESH
GROUP = QUERY_HEADS // KEY_VALUE_HEADS
GROUP_COLS = GROUP * HEAD_SIZE


def heads_kernel(
    q_in, k_in, v_in, cot_in, w_in, sid_in,
    dq_out, dk_out, dv_out, proj_out,
    cot, qg, kg, vg, sidg, wg, att, outb, acc, part, from_below, from_above, dqb, dkb, dvb,
    loc_sem, sid_s, sid_r, qkv_s, qkv_r, wp_s, wp_r, wu_s, wu_r, wd_s, wd_r,
    cot_s, cot_r, red_s, up_r, down_r, fin_s, fin_r, ret_s, ret_r,
):
    s = lax.axis_index("seq")
    d = lax.axis_index("dp")
    f = lax.axis_index("fsdp")
    length = qg.shape[0] // 4
    half = length // 2
    block = cot.shape[2]
    piece = block // 4
    factor = 1.0 / math.sqrt(HEAD_SIZE)

    def rows_of(side, window):
        return pl.ds(pl.multiple_of(window * length + side * half, half), half)

    def cols(index, width):
        return pl.ds(pl.multiple_of(index * width, width), width)

    def other(i):
        return lax.rem(f + i, 4)

    def source(i):
        return lax.rem(f + 4 - i, 4)

    def side(t):
        return s if t == 0 else 1 - s

    def remote(src, dst, send, recv, device):
        return pltpu.make_async_remote_copy(
            src_ref=src, dst_ref=dst, send_sem=send, recv_sem=recv,
            device_id=device, device_id_type=MESH,
        )

    pairs = [(t, i) for i in range(4) for t in range(2) if (t, i) != (0, 0)]
    beside = (1 - s, d, f)

    barrier = pltpu.get_barrier_semaphore()
    for t, i in pairs:
        pl.semaphore_signal(
            barrier, inc=1, device_id=(side(t), d, other(i)), device_id_type=MESH
        )

    @pl.when(d > 0)
    def _():
        pl.semaphore_signal(barrier, inc=1, device_id=(s, d - 1, f), device_id_type=MESH)

    @pl.when(d < 3)
    def _():
        pl.semaphore_signal(barrier, inc=1, device_id=(s, d + 1, f), device_id_type=MESH)

    pl.semaphore_wait(barrier, 8 + d * (3 - d) // 2)

    def weight_rows(plane, window):
        return pl.ds(pl.multiple_of((plane * 4 + window) * piece, piece), piece)

    def weight_copy(i, target, origin):
        return remote(
            w_in.at[:, cols(target, GROUP_COLS)], wg.at[weight_rows(d, origin)],
            wp_s.at[i], wp_r.at[i], (s, d, target),
        )

    for i in (1, 2, 3):
        weight_copy(i, other(i), f).start()
    own_weight = pltpu.make_async_copy(
        w_in.at[:, cols(f, GROUP_COLS)], wg.at[weight_rows(d, f)], loc_sem.at[0]
    )
    own_weight.start()

    def sid_copy(i, target, origin):
        return remote(sid_in, sidg.at[origin], sid_s.at[i], sid_r.at[i], (s, d, target))

    def own_or_sent(a, to_side, to_window, from_side, from_window):
        head = to_side * 4 + to_window
        src, dst, width = ((q_in, qg, GROUP_COLS), (k_in, kg, HEAD_SIZE), (v_in, vg, HEAD_SIZE))[a]
        return src.at[0, :, cols(head, width)], dst.at[rows_of(from_side, from_window)]

    def qkv_copy(a, t, i):
        src, dst = own_or_sent(a, side(t), other(i), s, f)
        return remote(src, dst, qkv_s.at[a, t, i], qkv_r.at[a, t, i], (side(t), d, other(i)))

    def qkv_arrival(a, t, i):
        src, dst = own_or_sent(a, s, f, side(t), source(i))
        return remote(src, dst, qkv_s.at[a, t, i], qkv_r.at[a, t, i], beside)

    local_copies = []
    for a in range(3):
        src, dst = own_or_sent(a, s, f, s, f)
        local_copies.append(pltpu.make_async_copy(src, dst, loc_sem.at[1 + a]))
    local_copies.append(pltpu.make_async_copy(sid_in, sidg.at[f], loc_sem.at[4]))
    for copy in local_copies:
        copy.start()
    for i in (1, 2, 3):
        sid_copy(i, other(i), f).start()
    for t, i in pairs:
        for a in range(3):
            qkv_copy(a, t, i).start()

    fy = lax.rem(f + 2, 4)
    fc = f + 1 - 2 * lax.rem(f, 2)
    fcy = lax.rem(fc + 2, 4)
    to_x, to_y, to_core = (1 - s, d, f), (s, d, fy), (s, d, fc)
    order = (3 * (1 - d // 2), lax.rem(12 - 2 * d, 5), 1 + lax.rem(d, 2), d)

    def span(from_side, window, part_of):
        start = window * length + from_side * half
        if part_of is None:
            return pl.ds(pl.multiple_of(start, half), half)
        quarter = half // 2
        return pl.ds(pl.multiple_of(start + part_of * quarter, quarter), quarter)

    kinds = (
        (to_x, (s, f, None), (1 - s, f, None)),
        (to_y, (s, f, None), (s, fy, None)),
        (to_core, (s, f, None), (s, fc, None)),
        (to_y, (1 - s, f, 0), (1 - s, fy, 0)),
        (to_core, (1 - s, f, None), (1 - s, fc, None)),
        (to_x, (s, fy, 1), (1 - s, fy, 1)),
        (to_core, (s, fy, None), (s, fcy, None)),
        (to_core, (1 - s, fy, 0), (1 - s, fcy, 0)),
        (to_core, (1 - s, fy, 1), (1 - s, fcy, 1)),
    )

    def cot_copy(j, kind):
        device, sent, _ = kinds[kind]
        dst = cot.at[order[j], span(*sent)]
        src = cot_in.at[0, :, cols(order[j], block)] if kind < 3 else dst
        return remote(src, dst, cot_s.at[kind, j], cot_r.at[kind, j], device)

    def cot_arrival(j, kind):
        device, _, came = kinds[kind]
        dst = cot.at[order[j], span(*came)]
        return remote(dst, dst, cot_s.at[kind, j], cot_r.at[kind, j], device)

    def own_cot(j):
        return pltpu.make_async_copy(
            cot_in.at[0, :, cols(order[j], block)], cot.at[order[j], span(s, f, None)],
            loc_sem.at[5 + j],
        )

    def cot_send(j):
        for kind in (0, 1, 2):
            cot_copy(j, kind).start()
        own_cot(j).start()

    def cot_pass(j):
        cot_arrival(j, 0).wait_recv()
        cot_copy(j, 3).start()
        cot_copy(j, 4).start()
        cot_arrival(j, 1).wait_recv()
        cot_copy(j, 5).start()
        cot_copy(j, 6).start()

    def cot_pass_on(j):
        cot_arrival(j, 3).wait_recv()
        cot_copy(j, 7).start()
        cot_arrival(j, 5).wait_recv()
        cot_copy(j, 8).start()

    def cot_ready(j):
        for kind in (2, 4, 6, 7, 8):
            cot_arrival(j, kind).wait_recv()
        own_cot(j).wait()

    def plane_rows(plane):
        return pl.ds(pl.multiple_of(plane * block, block), block)

    def weight_up(plane):
        ref = wg.at[plane_rows(plane)]
        return remote(ref, ref, wu_s.at[plane], wu_r.at[plane], (s, d + 1, f))

    def weight_down(plane):
        ref = wg.at[plane_rows(plane)]
        return remote(ref, ref, wd_s.at[plane], wd_r.at[plane], (s, d - 1, f))

    def weight_step(k):
        if k:
            @pl.when(d >= k)
            def _():
                weight_up(d - k).wait_recv()

        @pl.when((d >= k) & (d < 3))
        def _():
            weight_up(d - k).start()

        if k:
            @pl.when(d + k <= 3)
            def _():
                weight_down(d + k).wait_recv()

        @pl.when((d + k <= 3) & (d > 0))
        def _():
            weight_down(d + k).start()

    def forward(i, carry):
        window = lax.rem(f + 4 - i, 4)
        for a in range(3):
            @pl.when(i > 0)
            def _():
                qkv_arrival(a, 0, i).wait_recv()

            qkv_arrival(a, 1, i).wait_recv()

        @pl.when(i > 0)
        def _():
            sid_copy(i, fc, source(i)).wait_recv()

        rows = pl.ds(pl.multiple_of(window * length, length), length)
        keys = kg[rows, :]
        values = vg[rows, :]
        sent_key = jnp.broadcast_to(sidg[window][0:1, :], (length, length))
        sent_query = sent_key.T
        allowed = (sent_key <= sent_query) & (sent_key >= sent_query - 3.0)
        for h in range(GROUP):
            here = slice(h * HEAD_SIZE, (h + 1) * HEAD_SIZE)
            scores = factor * lax.dot_general(
                qg[rows, here], keys, (((1,), (1,)), ((), ())), preferred_element_type=jnp.float32
            )
            raised = jnp.where(allowed, jnp.exp(scores), 0.0)
            attend = raised * (1.0 / jnp.sum(raised, axis=1, keepdims=True))
            att[window * GROUP + h] = attend
            outb[rows, here] = jnp.dot(
                attend.astype(jnp.bfloat16), values, preferred_element_type=jnp.float32
            ).astype(jnp.bfloat16)
        return carry

    def slot_copy_up(slot):
        return remote(
            part.at[slot], from_below.at[slot], red_s.at[slot], up_r.at[slot], (s, d + 1, f)
        )

    def slot_copy_down(slot):
        return remote(
            part.at[slot], from_above.at[slot], red_s.at[slot], down_r.at[slot], (s, d - 1, f)
        )

    def final_copy(i, target, origin):
        return remote(
            part.at[d * 4 + target], proj_out.at[:, cols(origin, GROUP_COLS)],
            fin_s.at[i], fin_r.at[i], (s, d, target),
        )

    def own_final():
        return pltpu.make_async_copy(
            part.at[d * 4 + f], proj_out.at[:, cols(f, GROUP_COLS)], loc_sem.at[9]
        )

    def reduce_step(j):
        plane = order[j]

        def one(i, carry):
            r = lax.rem(f + i, 4)
            slot = plane * 4 + r
            acc[...] = lax.dot_general(
                cot[plane, :, cols(r, piece)], outb[...],
                (((0,), (0,)), ((), ())), preferred_element_type=jnp.float32,
            )

            @pl.when((plane >= d) & (d > 0))
            def _():
                slot_copy_up(slot).wait_recv()
                acc[...] += from_below[slot].astype(jnp.float32)

            @pl.when((plane <= d) & (d < 3))
            def _():
                slot_copy_down(slot).wait_recv()
                acc[...] += from_above[slot].astype(jnp.float32)

            part[slot] = acc[...].astype(jnp.bfloat16)
            if j < 3:
                @pl.when(plane > d)
                def _():
                    slot_copy_up(slot).start()

                @pl.when(plane < d)
                def _():
                    slot_copy_down(slot).start()
            else:
                @pl.when(i > 0)
                def _():
                    final_copy(i, r, f).start()

                @pl.when(i == 0)
                def _():
                    own_final().start()
            return carry

        lax.fori_loop(0, 4, one, 0)

    returned = ((dqb, dq_out, GROUP_COLS), (dkb, dk_out, HEAD_SIZE), (dvb, dv_out, HEAD_SIZE))

    def return_copy(a, t, i):
        buffer, out, width = returned[a]
        window = lax.rem(f + i, 4)
        return remote(
            buffer.at[rows_of(side(t), window)], out.at[0, :, cols(s * 4 + f, width)],
            ret_s.at[a, t, i], ret_r.at[a, t, i], (side(t), d, window),
        )

    def return_arrival(a, t, i):
        buffer, out, width = returned[a]
        return remote(
            buffer.at[rows_of(s, f)], out.at[0, :, cols(side(t) * 4 + source(i), width)],
            ret_s.at[a, t, i], ret_r.at[a, t, i], beside,
        )

    def own_return(a):
        buffer, out, width = returned[a]
        return pltpu.make_async_copy(
            buffer.at[rows_of(s, f)], out.at[0, :, cols(s * 4 + f, width)], loc_sem.at[10 + a]
        )

    def backward(i, carry):
        window = lax.rem(f + i, 4)
        rows = pl.ds(pl.multiple_of(window * length, length), length)
        upstream = jnp.zeros((length, GROUP_COLS), jnp.float32)
        for plane in range(4):
            upstream = upstream + jnp.dot(
                cot[plane, rows, :], wg[plane * block : (plane + 1) * block, :],
                preferred_element_type=jnp.float32,
            )
        upstream = upstream.astype(jnp.bfloat16)
        keys = kg[rows, :]
        values = vg[rows, :]
        key_sum = jnp.zeros((length, HEAD_SIZE), jnp.float32)
        value_sum = jnp.zeros((length, HEAD_SIZE), jnp.float32)
        for h in range(GROUP):
            here = slice(h * HEAD_SIZE, (h + 1) * HEAD_SIZE)
            attend = att[window * GROUP + h]
            upstream_head = upstream[:, here]
            grad_attend = lax.dot_general(
                upstream_head, values, (((1,), (1,)), ((), ())), preferred_element_type=jnp.float32
            )
            mean = jnp.sum(attend * grad_attend, axis=1, keepdims=True)
            dscore = (attend * (grad_attend - mean) * factor).astype(jnp.bfloat16)
            dqb[rows, here] = jnp.dot(
                dscore, keys, preferred_element_type=jnp.float32
            ).astype(jnp.bfloat16)
            key_sum = key_sum + lax.dot_general(
                dscore, qg[rows, here], (((0,), (0,)), ((), ())),
                preferred_element_type=jnp.float32,
            )
            value_sum = value_sum + lax.dot_general(
                attend.astype(jnp.bfloat16), upstream_head, (((0,), (0,)), ((), ())),
                preferred_element_type=jnp.float32,
            )
        dkb[rows, :] = key_sum.astype(jnp.bfloat16)
        dvb[rows, :] = value_sum.astype(jnp.bfloat16)
        for a in range(3):
            @pl.when(i > 0)
            def _():
                return_copy(a, 0, i).start()

            @pl.when(i == 0)
            def _():
                own_return(a).start()

            return_copy(a, 1, i).start()
        return carry

    own_weight.wait()
    for i in (1, 2, 3):
        weight_copy(i, fc, source(i)).wait_recv()
    weight_step(0)
    cot_send(0)
    cot_send(1)
    for copy in local_copies:
        copy.wait()
    lax.fori_loop(0, 4, forward, 0)
    cot_pass(0)
    cot_send(2)
    cot_pass_on(0)
    cot_pass(1)
    cot_ready(0)
    reduce_step(0)
    weight_step(1)
    cot_send(3)
    cot_pass_on(1)
    cot_pass(2)
    cot_ready(1)
    reduce_step(1)
    cot_pass_on(2)
    cot_pass(3)
    cot_ready(2)
    weight_step(2)
    reduce_step(2)
    cot_pass_on(3)
    cot_ready(3)

    @pl.when(d == 3)
    def _():
        weight_up(0).wait_recv()

    @pl.when(d == 0)
    def _():
        weight_down(3).wait_recv()

    lax.fori_loop(0, 4, backward, 0)
    reduce_step(3)

    for i in (1, 2, 3):
        weight_copy(i, other(i), f).wait_send()
        sid_copy(i, other(i), f).wait_send()
        final_copy(i, other(i), f).wait_send()
        final_copy(i, other(i), source(i)).wait_recv()
    own_final().wait()
    for a in range(3):
        own_return(a).wait()
        for t, i in pairs:
            qkv_copy(a, t, i).wait_send()
            return_copy(a, t, i).wait_send()
            return_arrival(a, t, i).wait_recv()
    for j in range(4):
        for kind in range(9):
            cot_copy(j, kind).wait_send()
    for k in range(3):
        @pl.when((d >= k) & (d < 3))
        def _():
            weight_up(d - k).wait_send()

        @pl.when((d + k <= 3) & (d > 0))
        def _():
            weight_down(d + k).wait_send()
    for j in range(3):
        def drain(i, carry):
            slot_copy_up(order[j] * 4 + lax.rem(f + i, 4)).wait_send()
            return carry

        lax.fori_loop(0, 4, drain, 0)


def per_device_heads(
    query_rows, forward_key_rows, forward_value_rows, out_cotangent, proj_weight, sent_lengths
):
    half, width = query_rows.shape[1:]
    length = 2 * half
    depth = proj_weight.shape[0]
    bounds = running_sums(sent_lengths[0])
    places = jnp.arange(length, dtype=jnp.int32)
    sentence = jnp.sum((places[None, :] >= bounds[:, None]).astype(jnp.float32), axis=0)
    sentence = jnp.broadcast_to(sentence[None, :], (8, length))
    block = out_cotangent.shape[2] // 4
    tokens = 4 * length
    bf16, f32 = jnp.bfloat16, jnp.float32
    dma = pltpu.SemaphoreType.DMA
    return pl.pallas_call(
        heads_kernel,
        out_shape=(
            jax.ShapeDtypeStruct(query_rows.shape, bf16),
            jax.ShapeDtypeStruct(forward_key_rows.shape, bf16),
            jax.ShapeDtypeStruct(forward_value_rows.shape, bf16),
            jax.ShapeDtypeStruct(proj_weight.shape, bf16),
        ),
        in_specs=[pl.BlockSpec(memory_space=pl.ANY)] * 6,
        out_specs=(pl.BlockSpec(memory_space=pl.ANY),) * 4,
        scratch_shapes=[
            pltpu.VMEM((4, tokens, block), bf16),
            pltpu.VMEM((tokens, GROUP_COLS), bf16),
            pltpu.VMEM((tokens, HEAD_SIZE), bf16),
            pltpu.VMEM((tokens, HEAD_SIZE), bf16),
            pltpu.VMEM((4, 8, length), f32),
            pltpu.VMEM((16 * depth, GROUP_COLS), bf16),
            pltpu.VMEM((4 * GROUP, length, length), f32),
            pltpu.VMEM((tokens, GROUP_COLS), bf16),
            pltpu.VMEM((depth, GROUP_COLS), f32),
            pltpu.VMEM((16, depth, GROUP_COLS), bf16),
            pltpu.VMEM((16, depth, GROUP_COLS), bf16),
            pltpu.VMEM((16, depth, GROUP_COLS), bf16),
            pltpu.VMEM((tokens, GROUP_COLS), bf16),
            pltpu.VMEM((tokens, HEAD_SIZE), bf16),
            pltpu.VMEM((tokens, HEAD_SIZE), bf16),
            dma((13,)),
            dma((4,)), dma((4,)),
            dma((3, 2, 4)), dma((3, 2, 4)),
            dma((4,)), dma((4,)),
            dma((4,)), dma((4,)), dma((4,)), dma((4,)),
            dma((9, 4)), dma((9, 4)),
            dma((16,)), dma((16,)), dma((16,)),
            dma((4,)), dma((4,)),
            dma((3, 2, 4)), dma((3, 2, 4)),
        ],
        compiler_params=pltpu.CompilerParams(
            collective_id=0, has_side_effects=True, vmem_limit_bytes=56 * 1024 * 1024
        ),
    )(query_rows, forward_key_rows, forward_value_rows, out_cotangent, proj_weight, sentence)


def solution(mesh):
    in_specs = (
        P(("dp", "fsdp"), "seq", None),
        P(("dp", "fsdp"), "seq", None),
        P(("dp", "fsdp"), "seq", None),
        P(("dp", "fsdp"), "seq", None),
        P(("dp", "fsdp"), "seq"),
        P(("dp", "fsdp"), None),
    )
    out_specs = (
        P(("dp", "fsdp"), "seq", None),
        P(("dp", "fsdp"), "seq", None),
        P(("dp", "fsdp"), "seq", None),
        P(("dp", "fsdp"), "seq"),
    )
    body = per_device
    if mesh.shape["seq"] == 2 and mesh.shape["dp"] == 4 and mesh.shape["fsdp"] == 4:
        body = per_device_heads
    return jax.shard_map(
        body, mesh=mesh, in_specs=in_specs, out_specs=out_specs, check_vma=False
    )
```

```python
import math

import jax
import jax.numpy as jnp
from jax import lax
from jax.experimental import pallas as pl
from jax.experimental.pallas import tpu as pltpu
from jax.sharding import PartitionSpec as P

QUERY_HEADS = 32
KEY_VALUE_HEADS = 8
HEAD_SIZE = 128


def running_sums(lengths):
    index = jnp.arange(lengths.shape[0], dtype=jnp.int32)
    return jnp.sum(jnp.where(index[None, :] <= index[:, None], lengths[None, :], 0), axis=1)


def per_device(
    query_rows, forward_key_rows, forward_value_rows, out_cotangent, proj_weight, sent_lengths
):
    queries_per_group = QUERY_HEADS // KEY_VALUE_HEADS
    factor = 1.0 / math.sqrt(HEAD_SIZE)
    gathered = lax.all_gather(out_cotangent, "seq", axis=1, tiled=True)
    cotangent = gathered[0]
    length = cotangent.shape[0]
    sliced = cotangent
    upstream_gradient = jnp.dot(
        sliced,
        lax.all_gather(proj_weight, ("dp", "fsdp"), axis=0, tiled=True),
        preferred_element_type=jnp.float32,
    ).astype(jnp.bfloat16)
    heads_of_queries, heads_of_keys, heads_of_values = (
        lax.all_to_all(query_rows, "seq", split_axis=2, concat_axis=1, tiled=True),
        lax.all_to_all(forward_key_rows, "seq", split_axis=2, concat_axis=1, tiled=True),
        lax.all_to_all(forward_value_rows, "seq", split_axis=2, concat_axis=1, tiled=True),
    )
    heads_of_queries = heads_of_queries[0]
    heads_of_keys = heads_of_keys[0]
    heads_of_values = heads_of_values[0]
    bounds = running_sums(sent_lengths[0])
    places = jnp.arange(length, dtype=jnp.int32)
    sentence = jnp.sum((places[:, None] >= bounds[None, :]).astype(jnp.int32), axis=1)
    block_rows = min(512, length)
    block_count = length // block_rows
    kv_local = heads_of_keys.shape[1] // HEAD_SIZE
    group_cols = queries_per_group * HEAD_SIZE
    output_parts = []
    query_parts = []
    key_parts = []
    value_parts = []
    for head_index in range(kv_local):
        key_head = heads_of_keys[:, head_index * HEAD_SIZE : (head_index + 1) * HEAD_SIZE]
        value_head = heads_of_values[:, head_index * HEAD_SIZE : (head_index + 1) * HEAD_SIZE]
        query_group = heads_of_queries[:, head_index * group_cols : (head_index + 1) * group_cols]
        upstream_group = upstream_gradient[
            :, head_index * group_cols : (head_index + 1) * group_cols
        ]

        def block_step(block_index, buffers):
            output_buf, query_buf, key_buf, value_buf = buffers
            offset = block_index * block_rows
            query_block = lax.dynamic_slice_in_dim(query_group, offset, block_rows, 0).reshape(
                block_rows, queries_per_group, HEAD_SIZE
            )
            upstream_block = lax.dynamic_slice_in_dim(
                upstream_group, offset, block_rows, 0
            ).reshape(block_rows, queries_per_group, HEAD_SIZE)
            sentence_query = lax.dynamic_slice_in_dim(sentence, offset, block_rows, 0)
            allowed = (sentence[None, :] <= sentence_query[:, None]) & (
                sentence[None, :] >= sentence_query[:, None] - 3
            )
            scores = (
                jnp.einsum("qhd,kd->hqk", query_block, key_head, preferred_element_type=jnp.float32)
                * factor
            )
            raised = jnp.where(allowed[None], jnp.exp(scores), 0.0)
            attend = raised / jnp.sum(raised, axis=-1, keepdims=True)
            rounded = attend.astype(jnp.bfloat16)
            output_block = jnp.einsum(
                "hqk,kd->qhd", rounded, value_head, preferred_element_type=jnp.float32
            ).astype(jnp.bfloat16)
            grad_attend = jnp.einsum(
                "qhd,kd->hqk", upstream_block, value_head, preferred_element_type=jnp.float32
            )
            dscore = (
                attend
                * (grad_attend - jnp.sum(attend * grad_attend, axis=-1, keepdims=True))
                * factor
            ).astype(jnp.bfloat16)
            query_block_grad = jnp.einsum(
                "hqk,kd->qhd", dscore, key_head, preferred_element_type=jnp.float32
            ).astype(jnp.bfloat16)
            key_window_grad = jnp.einsum(
                "hqk,qhd->kd", dscore, query_block, preferred_element_type=jnp.float32
            )
            value_window_grad = jnp.einsum(
                "hqk,qhd->kd", rounded, upstream_block, preferred_element_type=jnp.float32
            )
            output_buf = lax.dynamic_update_slice_in_dim(
                output_buf, output_block.reshape(block_rows, group_cols), offset, 0
            )
            query_buf = lax.dynamic_update_slice_in_dim(
                query_buf, query_block_grad.reshape(block_rows, group_cols), offset, 0
            )
            key_old = key_buf
            key_buf = key_old + key_window_grad
            value_old = value_buf
            value_buf = value_old + value_window_grad
            return (output_buf, query_buf, key_buf, value_buf)

        starting = (
            jnp.zeros((length, group_cols), jnp.bfloat16),
            jnp.zeros((length, group_cols), jnp.bfloat16),
            jnp.zeros((length, HEAD_SIZE), jnp.float32),
            jnp.zeros((length, HEAD_SIZE), jnp.float32),
        )
        output_buf, query_buf, key_buf, value_buf = lax.fori_loop(
            0, block_count, block_step, starting
        )
        output_parts.append(output_buf)
        query_parts.append(query_buf)
        key_parts.append(key_buf.astype(jnp.bfloat16))
        value_parts.append(value_buf.astype(jnp.bfloat16))
    output_all = jnp.concatenate(output_parts, axis=1)
    query_all = jnp.concatenate(query_parts, axis=1)
    key_all = jnp.concatenate(key_parts, axis=1)
    value_all = jnp.concatenate(value_parts, axis=1)
    sliced = cotangent
    proj_grad = lax.psum_scatter(
        lax.dot_general(
            sliced, output_all, (((0,), (0,)), ((), ())), preferred_element_type=jnp.float32
        ),
        ("dp", "fsdp"),
        scatter_dimension=0,
        tiled=True,
    ).astype(jnp.bfloat16)
    query_grad, key_gradient, value_gradient = (
        lax.all_to_all(query_all[None], "seq", split_axis=1, concat_axis=2, tiled=True),
        lax.all_to_all(key_all[None], "seq", split_axis=1, concat_axis=2, tiled=True),
        lax.all_to_all(value_all[None], "seq", split_axis=1, concat_axis=2, tiled=True),
    )
    return (query_grad, key_gradient, value_gradient, proj_grad)


MESH = pl.DeviceIdType.MESH
GROUP = QUERY_HEADS // KEY_VALUE_HEADS
GROUP_COLS = GROUP * HEAD_SIZE


def heads_kernel(
    q_in, k_in, v_in, cot_in, w_in, sid_in,
    dq_out, dk_out, dv_out, proj_out,
    cot, qg, kg, vg, sidg, wg, att, outb, acc, part, from_below, from_above, dqb, dkb, dvb,
    loc_sem, sid_s, sid_r, qkv_s, qkv_r, wp_s, wp_r, wu_s, wu_r, wd_s, wd_r,
    cot_s, cot_r, red_s, up_r, down_r, fin_s, fin_r, ret_s, ret_r,
):
    s = lax.axis_index("seq")
    d = lax.axis_index("dp")
    f = lax.axis_index("fsdp")
    length = qg.shape[0] // 4
    half = length // 2
    block = cot.shape[2]
    piece = block // 4
    factor = 1.0 / math.sqrt(HEAD_SIZE)

    def rows_of(side, window):
        return pl.ds(pl.multiple_of(window * length + side * half, half), half)

    def cols(index, width):
        return pl.ds(pl.multiple_of(index * width, width), width)

    def other(i):
        return lax.rem(f + i, 4)

    def source(i):
        return lax.rem(f + 4 - i, 4)

    def side(t):
        return s if t == 0 else 1 - s

    def remote(src, dst, send, recv, device):
        return pltpu.make_async_remote_copy(
            src_ref=src, dst_ref=dst, send_sem=send, recv_sem=recv,
            device_id=device, device_id_type=MESH,
        )

    pairs = [(t, i) for i in range(4) for t in range(2) if (t, i) != (0, 0)]
    beside = (1 - s, d, f)

    barrier = pltpu.get_barrier_semaphore()
    for t, i in pairs:
        pl.semaphore_signal(
            barrier, inc=1, device_id=(side(t), d, other(i)), device_id_type=MESH
        )

    @pl.when(d > 0)
    def _():
        pl.semaphore_signal(barrier, inc=1, device_id=(s, d - 1, f), device_id_type=MESH)

    @pl.when(d < 3)
    def _():
        pl.semaphore_signal(barrier, inc=1, device_id=(s, d + 1, f), device_id_type=MESH)

    pl.semaphore_wait(barrier, 8 + d * (3 - d) // 2)

    def weight_rows(plane, window):
        return pl.ds(pl.multiple_of((plane * 4 + window) * piece, piece), piece)

    def weight_copy(i, target, origin):
        return remote(
            w_in.at[:, cols(target, GROUP_COLS)], wg.at[weight_rows(d, origin)],
            wp_s.at[i], wp_r.at[i], (s, d, target),
        )

    for i in (1, 2, 3):
        weight_copy(i, other(i), f).start()
    own_weight = pltpu.make_async_copy(
        w_in.at[:, cols(f, GROUP_COLS)], wg.at[weight_rows(d, f)], loc_sem.at[0]
    )
    own_weight.start()

    def sid_copy(i, target, origin):
        return remote(sid_in, sidg.at[origin], sid_s.at[i], sid_r.at[i], (s, d, target))

    def own_or_sent(a, to_side, to_window, from_side, from_window):
        head = to_side * 4 + to_window
        src, dst, width = ((q_in, qg, GROUP_COLS), (k_in, kg, HEAD_SIZE), (v_in, vg, HEAD_SIZE))[a]
        return src.at[0, :, cols(head, width)], dst.at[rows_of(from_side, from_window)]

    def qkv_copy(a, t, i):
        src, dst = own_or_sent(a, side(t), other(i), s, f)
        return remote(src, dst, qkv_s.at[a, t, i], qkv_r.at[a, t, i], (side(t), d, other(i)))

    def qkv_arrival(a, t, i):
        src, dst = own_or_sent(a, s, f, side(t), source(i))
        return remote(src, dst, qkv_s.at[a, t, i], qkv_r.at[a, t, i], beside)

    local_copies = []
    for a in range(3):
        src, dst = own_or_sent(a, s, f, s, f)
        local_copies.append(pltpu.make_async_copy(src, dst, loc_sem.at[1 + a]))
    local_copies.append(pltpu.make_async_copy(sid_in, sidg.at[f], loc_sem.at[4]))
    for copy in local_copies:
        copy.start()
    for i in (1, 2, 3):
        sid_copy(i, other(i), f).start()
    for t, i in pairs:
        for a in range(3):
            qkv_copy(a, t, i).start()

    fy = lax.rem(f + 2, 4)
    fc = f + 1 - 2 * lax.rem(f, 2)
    fcy = lax.rem(fc + 2, 4)
    to_x, to_y, to_core = (1 - s, d, f), (s, d, fy), (s, d, fc)
    order = (3 * (1 - d // 2), lax.rem(12 - 2 * d, 5), 1 + lax.rem(d, 2), d)

    def span(from_side, window, part_of):
        start = window * length + from_side * half
        if part_of is None:
            return pl.ds(pl.multiple_of(start, half), half)
        quarter = half // 2
        return pl.ds(pl.multiple_of(start + part_of * quarter, quarter), quarter)

    kinds = (
        (to_x, (s, f, None), (1 - s, f, None)),
        (to_y, (s, f, None), (s, fy, None)),
        (to_core, (s, f, None), (s, fc, None)),
        (to_y, (1 - s, f, 0), (1 - s, fy, 0)),
        (to_core, (1 - s, f, None), (1 - s, fc, None)),
        (to_x, (s, fy, 1), (1 - s, fy, 1)),
        (to_core, (s, fy, None), (s, fcy, None)),
        (to_core, (1 - s, fy, 0), (1 - s, fcy, 0)),
        (to_core, (1 - s, fy, 1), (1 - s, fcy, 1)),
    )

    def cot_copy(j, kind):
        device, sent, _ = kinds[kind]
        dst = cot.at[order[j], span(*sent)]
        src = cot_in.at[0, :, cols(order[j], block)] if kind < 3 else dst
        return remote(src, dst, cot_s.at[kind, j], cot_r.at[kind, j], device)

    def cot_arrival(j, kind):
        device, _, came = kinds[kind]
        dst = cot.at[order[j], span(*came)]
        return remote(dst, dst, cot_s.at[kind, j], cot_r.at[kind, j], device)

    def own_cot(j):
        return pltpu.make_async_copy(
            cot_in.at[0, :, cols(order[j], block)], cot.at[order[j], span(s, f, None)],
            loc_sem.at[5 + j],
        )

    def cot_send(j):
        for kind in (0, 1, 2):
            cot_copy(j, kind).start()
        own_cot(j).start()

    def cot_pass(j):
        cot_arrival(j, 0).wait_recv()
        cot_copy(j, 3).start()
        cot_copy(j, 4).start()
        cot_arrival(j, 1).wait_recv()
        cot_copy(j, 5).start()
        cot_copy(j, 6).start()

    def cot_pass_on(j):
        cot_arrival(j, 3).wait_recv()
        cot_copy(j, 7).start()
        cot_arrival(j, 5).wait_recv()
        cot_copy(j, 8).start()

    def cot_ready(j):
        for kind in (2, 4, 6, 7, 8):
            cot_arrival(j, kind).wait_recv()
        own_cot(j).wait()

    def plane_rows(plane):
        return pl.ds(pl.multiple_of(plane * block, block), block)

    def weight_up(plane):
        ref = wg.at[plane_rows(plane)]
        return remote(ref, ref, wu_s.at[plane], wu_r.at[plane], (s, d + 1, f))

    def weight_down(plane):
        ref = wg.at[plane_rows(plane)]
        return remote(ref, ref, wd_s.at[plane], wd_r.at[plane], (s, d - 1, f))

    def weight_step(k):
        if k:
            @pl.when(d >= k)
            def _():
                weight_up(d - k).wait_recv()

        @pl.when((d >= k) & (d < 3))
        def _():
            weight_up(d - k).start()

        if k:
            @pl.when(d + k <= 3)
            def _():
                weight_down(d + k).wait_recv()

        @pl.when((d + k <= 3) & (d > 0))
        def _():
            weight_down(d + k).start()

    def forward(i, carry):
        window = lax.rem(f + 4 - i, 4)
        for a in range(3):
            @pl.when(i > 0)
            def _():
                qkv_arrival(a, 0, i).wait_recv()

            qkv_arrival(a, 1, i).wait_recv()

        @pl.when(i > 0)
        def _():
            sid_copy(i, fc, source(i)).wait_recv()

        rows = pl.ds(pl.multiple_of(window * length, length), length)
        keys = kg[rows, :]
        values = vg[rows, :]
        sent_key = jnp.broadcast_to(sidg[window][0:1, :], (length, length))
        sent_query = sent_key.T
        allowed = (sent_key <= sent_query) & (sent_key >= sent_query - 3.0)
        for h in range(GROUP):
            here = slice(h * HEAD_SIZE, (h + 1) * HEAD_SIZE)
            scores = factor * lax.dot_general(
                qg[rows, here], keys, (((1,), (1,)), ((), ())), preferred_element_type=jnp.float32
            )
            raised = jnp.where(allowed, jnp.exp(scores), 0.0)
            attend = raised * (1.0 / jnp.sum(raised, axis=1, keepdims=True))
            att[window * GROUP + h] = attend
            outb[rows, here] = jnp.dot(
                attend.astype(jnp.bfloat16), values, preferred_element_type=jnp.float32
            ).astype(jnp.bfloat16)
        return carry

    def slot_copy_up(slot):
        return remote(
            part.at[slot], from_below.at[slot], red_s.at[slot], up_r.at[slot], (s, d + 1, f)
        )

    def slot_copy_down(slot):
        return remote(
            part.at[slot], from_above.at[slot], red_s.at[slot], down_r.at[slot], (s, d - 1, f)
        )

    def final_copy(i, target, origin):
        return remote(
            part.at[d * 4 + target], proj_out.at[:, cols(origin, GROUP_COLS)],
            fin_s.at[i], fin_r.at[i], (s, d, target),
        )

    def own_final():
        return pltpu.make_async_copy(
            part.at[d * 4 + f], proj_out.at[:, cols(f, GROUP_COLS)], loc_sem.at[9]
        )

    def reduce_step(j):
        plane = order[j]

        def one(i, carry):
            r = lax.rem(f + i, 4)
            slot = plane * 4 + r
            acc[...] = lax.dot_general(
                cot[plane, :, cols(r, piece)], outb[...],
                (((0,), (0,)), ((), ())), preferred_element_type=jnp.float32,
            )

            @pl.when((plane >= d) & (d > 0))
            def _():
                slot_copy_up(slot).wait_recv()
                acc[...] += from_below[slot].astype(jnp.float32)

            @pl.when((plane <= d) & (d < 3))
            def _():
                slot_copy_down(slot).wait_recv()
                acc[...] += from_above[slot].astype(jnp.float32)

            part[slot] = acc[...].astype(jnp.bfloat16)
            if j < 3:
                @pl.when(plane > d)
                def _():
                    slot_copy_up(slot).start()

                @pl.when(plane < d)
                def _():
                    slot_copy_down(slot).start()
            else:
                @pl.when(i > 0)
                def _():
                    final_copy(i, r, f).start()

                @pl.when(i == 0)
                def _():
                    own_final().start()
            return carry

        lax.fori_loop(0, 4, one, 0)

    returned = ((dqb, dq_out, GROUP_COLS), (dkb, dk_out, HEAD_SIZE), (dvb, dv_out, HEAD_SIZE))

    def return_copy(a, t, i):
        buffer, out, width = returned[a]
        window = lax.rem(f + i, 4)
        return remote(
            buffer.at[rows_of(side(t), window)], out.at[0, :, cols(s * 4 + f, width)],
            ret_s.at[a, t, i], ret_r.at[a, t, i], (side(t), d, window),
        )

    def return_arrival(a, t, i):
        buffer, out, width = returned[a]
        return remote(
            buffer.at[rows_of(s, f)], out.at[0, :, cols(side(t) * 4 + source(i), width)],
            ret_s.at[a, t, i], ret_r.at[a, t, i], beside,
        )

    def own_return(a):
        buffer, out, width = returned[a]
        return pltpu.make_async_copy(
            buffer.at[rows_of(s, f)], out.at[0, :, cols(s * 4 + f, width)], loc_sem.at[10 + a]
        )

    def backward(i, carry):
        window = lax.rem(f + i, 4)
        rows = pl.ds(pl.multiple_of(window * length, length), length)
        upstream = jnp.zeros((length, GROUP_COLS), jnp.float32)
        for plane in range(4):
            upstream = upstream + jnp.dot(
                cot[plane, rows, :], wg[plane * block : (plane + 1) * block, :],
                preferred_element_type=jnp.float32,
            )
        upstream = upstream.astype(jnp.bfloat16)
        keys = kg[rows, :]
        values = vg[rows, :]
        key_sum = jnp.zeros((length, HEAD_SIZE), jnp.float32)
        value_sum = jnp.zeros((length, HEAD_SIZE), jnp.float32)
        for h in range(GROUP):
            here = slice(h * HEAD_SIZE, (h + 1) * HEAD_SIZE)
            attend = att[window * GROUP + h]
            upstream_head = upstream[:, here]
            grad_attend = lax.dot_general(
                upstream_head, values, (((1,), (1,)), ((), ())), preferred_element_type=jnp.float32
            )
            mean = jnp.sum(attend * grad_attend, axis=1, keepdims=True)
            dscore = (attend * (grad_attend - mean) * factor).astype(jnp.bfloat16)
            dqb[rows, here] = jnp.dot(
                dscore, keys, preferred_element_type=jnp.float32
            ).astype(jnp.bfloat16)
            key_sum = key_sum + lax.dot_general(
                dscore, qg[rows, here], (((0,), (0,)), ((), ())),
                preferred_element_type=jnp.float32,
            )
            value_sum = value_sum + lax.dot_general(
                attend.astype(jnp.bfloat16), upstream_head, (((0,), (0,)), ((), ())),
                preferred_element_type=jnp.float32,
            )
        dkb[rows, :] = key_sum.astype(jnp.bfloat16)
        dvb[rows, :] = value_sum.astype(jnp.bfloat16)
        for a in range(3):
            @pl.when(i > 0)
            def _():
                return_copy(a, 0, i).start()

            @pl.when(i == 0)
            def _():
                own_return(a).start()

            return_copy(a, 1, i).start()
        return carry

    own_weight.wait()
    for i in (1, 2, 3):
        weight_copy(i, fc, source(i)).wait_recv()
    weight_step(0)
    cot_send(0)
    cot_send(1)
    for copy in local_copies: copy.wait()
    lax.fori_loop(0, 4, forward, 0)
    cot_pass(0)
    cot_send(2)
    cot_pass(1)
    cot_pass_on(0)
    weight_step(1)
    cot_send(3)
    cot_ready(0)
    reduce_step(0)
    cot_pass_on(1)
    cot_pass(2)
    cot_ready(1)
    weight_step(2)
    cot_pass_on(2)
    cot_pass(3)
    cot_pass_on(3)
    reduce_step(1)
    cot_ready(2)
    reduce_step(2)
    cot_ready(3)

    @pl.when(d == 3)
    def _():
        weight_up(0).wait_recv()

    @pl.when(d == 0)
    def _():
        weight_down(3).wait_recv()

    lax.fori_loop(0, 4, backward, 0)
    reduce_step(3)

    for i in (1, 2, 3):
        weight_copy(i, other(i), f).wait_send()
        sid_copy(i, other(i), f).wait_send()
        final_copy(i, other(i), f).wait_send()
        final_copy(i, other(i), source(i)).wait_recv()
    own_final().wait()
    for a in range(3):
        own_return(a).wait()
        for t, i in pairs:
            qkv_copy(a, t, i).wait_send()
            return_copy(a, t, i).wait_send()
            return_arrival(a, t, i).wait_recv()
    for j in range(4):
        for kind in range(9):
            cot_copy(j, kind).wait_send()
    for k in range(3):
        @pl.when((d >= k) & (d < 3))
        def _():
            weight_up(d - k).wait_send()

        @pl.when((d + k <= 3) & (d > 0))
        def _():
            weight_down(d + k).wait_send()
    for j in range(3):
        def drain(i, carry):
            slot_copy_up(order[j] * 4 + lax.rem(f + i, 4)).wait_send()
            return carry

        lax.fori_loop(0, 4, drain, 0)


def per_device_heads(
    query_rows, forward_key_rows, forward_value_rows, out_cotangent, proj_weight, sent_lengths
):
    half, width = query_rows.shape[1:]
    length = 2 * half
    depth = proj_weight.shape[0]
    bounds = running_sums(sent_lengths[0])
    places = jnp.arange(length, dtype=jnp.int32)
    sentence = jnp.sum((places[None, :] >= bounds[:, None]).astype(jnp.float32), axis=0)
    sentence = jnp.broadcast_to(sentence[None, :], (8, length))
    block = out_cotangent.shape[2] // 4
    tokens = 4 * length
    bf16, f32 = jnp.bfloat16, jnp.float32
    dma = pltpu.SemaphoreType.DMA
    return pl.pallas_call(
        heads_kernel,
        out_shape=(
            jax.ShapeDtypeStruct(query_rows.shape, bf16),
            jax.ShapeDtypeStruct(forward_key_rows.shape, bf16),
            jax.ShapeDtypeStruct(forward_value_rows.shape, bf16),
            jax.ShapeDtypeStruct(proj_weight.shape, bf16),
        ),
        in_specs=[pl.BlockSpec(memory_space=pl.ANY)] * 6,
        out_specs=(pl.BlockSpec(memory_space=pl.ANY),) * 4,
        scratch_shapes=[
            pltpu.VMEM((4, tokens, block), bf16),
            pltpu.VMEM((tokens, GROUP_COLS), bf16),
            pltpu.VMEM((tokens, HEAD_SIZE), bf16),
            pltpu.VMEM((tokens, HEAD_SIZE), bf16),
            pltpu.VMEM((4, 8, length), f32),
            pltpu.VMEM((16 * depth, GROUP_COLS), bf16),
            pltpu.VMEM((4 * GROUP, length, length), f32),
            pltpu.VMEM((tokens, GROUP_COLS), bf16),
            pltpu.VMEM((depth, GROUP_COLS), f32),
            pltpu.VMEM((16, depth, GROUP_COLS), bf16),
            pltpu.VMEM((16, depth, GROUP_COLS), bf16),
            pltpu.VMEM((16, depth, GROUP_COLS), bf16),
            pltpu.VMEM((tokens, GROUP_COLS), bf16),
            pltpu.VMEM((tokens, HEAD_SIZE), bf16),
            pltpu.VMEM((tokens, HEAD_SIZE), bf16),
            dma((13,)),
            dma((4,)), dma((4,)),
            dma((3, 2, 4)), dma((3, 2, 4)),
            dma((4,)), dma((4,)),
            dma((4,)), dma((4,)), dma((4,)), dma((4,)),
            dma((9, 4)), dma((9, 4)),
            dma((16,)), dma((16,)), dma((16,)),
            dma((4,)), dma((4,)),
            dma((3, 2, 4)), dma((3, 2, 4)),
        ],
        compiler_params=pltpu.CompilerParams(
            collective_id=0, has_side_effects=True, vmem_limit_bytes=56 * 1024 * 1024
        ),
    )(query_rows, forward_key_rows, forward_value_rows, out_cotangent, proj_weight, sentence)


def solution(mesh):
    in_specs = (
        P(("dp", "fsdp"), "seq", None),
        P(("dp", "fsdp"), "seq", None),
        P(("dp", "fsdp"), "seq", None),
        P(("dp", "fsdp"), "seq", None),
        P(("dp", "fsdp"), "seq"),
        P(("dp", "fsdp"), None),
    )
    out_specs = (
        P(("dp", "fsdp"), "seq", None),
        P(("dp", "fsdp"), "seq", None),
        P(("dp", "fsdp"), "seq", None),
        P(("dp", "fsdp"), "seq"),
    )
    body = per_device
    if mesh.shape["seq"] == 2 and mesh.shape["dp"] == 4 and mesh.shape["fsdp"] == 4:
        body = per_device_heads
    return jax.shard_map(
        body, mesh=mesh, in_specs=in_specs, out_specs=out_specs, check_vma=False
    )
```
